32 devices in a mesh: seq: 4 (over y, x), exp: 8 (over z, core).
Axes of the slice: x: 2, y: 2, z: 4, core: 2. Of those that a mesh axis runs over, the one named last changes fastest.
Arguments:
- resid: bfloat16 [8, 384, 2048], P('exp', 'seq'), may hold values from -6 to 6
- qkv: bfloat16 [8, 384, 6144], P('exp', 'seq'), may hold values from -8 to 8
- w_out: bfloat16 [2048, 2048], P('seq'), may hold values from -0.125 to 0.125
- norm_gain: float32 [2048], replicated, may hold values from 0.1 to 1.9
- router_w: bfloat16 [2048, 64], replicated, may hold values from -0.125 to 0.125
- expert_ids: int32 [8, 384, 6], P('exp'), may hold values from 0 to 63, all different within a row; in each aligned block of 96 rows (0 to 95, 96 to 191, ..., all dimensions but the last counted through in order) at most 12 rows name the same one
- w_gate_up: bfloat16 [64, 2048, 2, 1408], P('exp', None, None, 'seq'), may hold values from -0.125 to 0.125
- w_down: bfloat16 [64, 1408, 2048], P('exp', 'seq'), may hold values from -0.15625 to 0.15625
Outputs:
- layer_out: bfloat16 [8, 384, 2048], P('exp', 'seq')
The draws below stay inside these ranges and needn't reach their ends.
Inputs may be any that keep to these rules, and one draw needn't show every extreme that they name: `expert_ids`: each point names 6 different experts. In each aligned block of 96 points (the points of one device, in the order of sets and then points), no expert is named by more than 12 points, and in every draw some expert is named by exactly 12 points of some block.
All inputs are finite; a program needn't handle non-finite values.
Results may differ from the reference program's by a relative error of at most 0.0065.
Values may be sent and summed in bfloat16 or wider, within the bound.
A program may use at most 128 MiB of HBM per device.

```python
import math
import jax
import jax.numpy as jnp
import numpy as np
from jax import lax

D = 2048
H = 16
HD = 128
FF = 1408
EXPERTS = 64
TOPK = 6
TOK_DEV = 96
SET_LEN = 384
SETS = 8
SLOTS = 12
N_SEQ = 4


def draw_qkv(key, part):
    base = jnp.clip(jax.random.normal(key, (SETS, SET_LEN, 3, D), jnp.float32), -8.0, 8.0)
    return base.reshape(SETS, SET_LEN, 3 * D).astype(jnp.bfloat16)


def level_of(stream_key, dims, shards, low, top_value):
    factor_of = 1.0
    for axis_at, blocks in shards:
        draws = jax.random.uniform(jax.random.fold_in(jax.random.fold_in(stream_key, 6), axis_at), (blocks,), jnp.float32, low / len(shards), top_value / len(shards))
        factor_of = factor_of * jnp.repeat(jnp.exp(draws), dims[axis_at] // blocks).reshape((-1,) + (1,) * (len(dims) - 1 - axis_at))
    return factor_of


def routed_block(stream_key, own, number, rows, number_of, top, limit, slope):
    ranking = jax.random.permutation(stream_key, number_of)
    crowded, common = load_shares(number_of, rows * top, limit, slope, True), load_shares(number_of, rows * top, limit, slope, False)
    places = jnp.arange(number_of)

    def named(sizes, offset_by):
        used = int((sizes > 0).sum())
        fixed = max(1, used // 4)
        moved = fixed + (places - fixed + offset_by * (used - fixed)) % max(1, number_of - fixed)
        return jnp.zeros((number_of,), jnp.int32).at[ranking[jnp.where(places < fixed, places, moved)]].set(jnp.asarray(sizes, jnp.int32))

    sizes = jnp.where(number % 4 == 0, named(crowded, number // 4), named(common, number - number // 4 - 1))
    mixed = jax.random.permutation(jax.random.fold_in(own, 3), number_of)
    giver, receiver = mixed[0:number_of // 2 * 2:2], mixed[1:number_of // 2 * 2:2]
    slack = jnp.minimum(sizes[giver] - 1, limit - sizes[receiver]) // 2
    slack = jnp.where((giver == ranking[0]) | (receiver == ranking[0]) | (sizes[receiver] == 0), 0, jnp.maximum(slack, 0))
    moved = jax.random.randint(jax.random.fold_in(own, 4), (number_of // 2,), 0, 1 << 20) % (slack + 1)
    sizes = sizes.at[giver].add(-moved).at[receiver].add(moved)
    labels = jnp.searchsorted(jnp.cumsum(sizes), jnp.arange(rows * top), side="right").astype(jnp.int32)
    grid = labels.reshape(top, rows).T
    grid = grid[jax.random.permutation(jax.random.fold_in(own, 1), rows)]
    offset_by = jax.random.randint(jax.random.fold_in(own, 2), (rows, 1), 0, top)
    return jnp.take_along_axis(grid, (jnp.arange(top)[None, :] + offset_by) % top, axis=1)


def load_shares(count, total, most, slope, full):
    loads = [(1 << 20) // math.isqrt(standing ** slope) + 1 for standing in range(1, count + 1)]
    largest = most if full else min(most, max(-(-total // count), total * loads[0] // sum(loads)))
    least = 1 if total - largest >= count - 1 else 0
    counts, surplus = [largest] + [least] * (count - 1), total - largest - least * (count - 1)
    while surplus > 0:
        free = [i for i in range(1, count) if counts[i] < largest] or [i for i in range(1, count) if counts[i] < most]
        whole, remaining = sum([loads[i] for i in free]), surplus
        for i in free:
            more = min(most - counts[i], max(1, remaining * loads[i] // whole), surplus)
            counts[i] = counts[i] + more
            surplus = surplus - more
    return np.array(counts)


def normal_values(key, dims, scale, limit, split=(), kind=jnp.bfloat16):
    factor_of = level_of(key, dims, split, -0.22, 0.18) if split else 1.0
    result = jax.random.normal(key, dims, jnp.float32) * scale * factor_of
    return jnp.minimum(jnp.maximum(result, -limit), limit).astype(kind)


def setup_inputs(seed: int = 0) -> dict:
    key_of = jax.random.split(jax.random.key(seed), 9)
    resid = normal_values(key_of[0], (SETS, SET_LEN, D), 1.0, 6.0, ((0, 8), (1, 4)))
    qkv = draw_qkv(jax.random.fold_in(key_of[8], 71), 0)
    w_out = normal_values(key_of[2], (D, D), D ** -0.5, 0.125, ((0, 4),))
    norm_gain = jnp.clip(1.0 + 0.18 * jax.random.normal(key_of[3], (D,), jnp.float32), 0.1, 1.9)
    router_w = normal_values(key_of[4], (D, EXPERTS), D ** -0.5, 0.125)
    expert_ids_keys = jax.random.split(jax.random.fold_in(key_of[5], 1), SETS * SET_LEN // TOK_DEV)
    expert_ids_turns = jax.random.permutation(jax.random.fold_in(key_of[5], 3), SETS * SET_LEN // TOK_DEV)
    expert_ids = jax.vmap(lambda own, number: routed_block(jax.random.fold_in(key_of[5], 2), own, number, TOK_DEV, EXPERTS, TOPK, SLOTS, 2))(expert_ids_keys, expert_ids_turns).reshape((SETS, SET_LEN, TOPK))
    w_gate_up = normal_values(key_of[6], (EXPERTS, D, 2, FF), D ** -0.5, 0.125, ((0, 8), (3, 4)))
    w_down = normal_values(key_of[7], (EXPERTS, FF, D), FF ** -0.5, 0.15625, ((0, 8), (1, 4)))
    return {"resid": resid, "qkv": qkv, "w_out": w_out, "norm_gain": norm_gain, "router_w": router_w, "expert_ids": expert_ids, "w_gate_up": w_gate_up, "w_down": w_down}


epsilon = 1e-05

def gate_weights(normed_rows, router_w, chosen):
    logits = jnp.dot(normed_rows, router_w, preferred_element_type=jnp.float32)
    match = chosen[:, :, None] == jnp.arange(logits.shape[1], dtype=jnp.int32)[None, None, :]
    picked = lax.optimization_barrier(jnp.sum(jnp.where(match, logits[:, None, :], jnp.zeros((), logits.dtype)), axis=-1))
    squashed = jax.nn.sigmoid(picked)
    return squashed / lax.optimization_barrier(jnp.sum(squashed, axis=-1, keepdims=True))

def slot_ranks(chosen, block_rows, experts):
    blocks = chosen.shape[0] // block_rows
    grouped = chosen.reshape(blocks, block_rows * chosen.shape[1])
    hits = (grouped[:, :, None] == jnp.arange(experts, dtype=jnp.int32)[None, None, :]).astype(jnp.int32)
    ranks = lax.optimization_barrier(jnp.sum(jnp.cumsum(hits, axis=1) * hits, axis=-1)) - 1
    return ranks.reshape(chosen.shape).astype(jnp.int32)

def attend(set_block):
    parts = set_block.reshape(SET_LEN, 3, H, HD).astype(jnp.float32)
    scores = jnp.einsum('qhd,khd->hqk', parts[:, 0], parts[:, 1]) / math.sqrt(HD)
    rounded = jax.nn.softmax(scores, axis=-1).astype(jnp.bfloat16)
    weights = lax.optimization_barrier(rounded).astype(jnp.float32)
    mixed = jnp.einsum('hqk,khd->qhd', weights, parts[:, 2])
    return mixed.reshape(SET_LEN, D).astype(jnp.bfloat16)

def expert_out(packed):
    inputs, gate_up, down = packed
    count_rows = inputs.shape[0]
    both = jnp.dot(inputs, gate_up.reshape(D, 2 * FF), preferred_element_type=jnp.float32).reshape(count_rows, 2, FF)
    hidden = (jax.nn.silu(both[:, 0]) * both[:, 1]).astype(jnp.bfloat16)
    block_units = FF // N_SEQ
    running = jnp.zeros((count_rows, D), jnp.float32)
    for quarter in range(N_SEQ):
        lower = quarter * block_units
        part_out = jnp.dot(hidden[:, lower:lower + block_units], down[lower:lower + block_units], preferred_element_type=jnp.float32).astype(jnp.bfloat16)
        running = running + lax.optimization_barrier(part_out).astype(jnp.float32)
    return running

def reference(resid, qkv, w_out, norm_gain, router_w, expert_ids, w_gate_up, w_down):
    attended = lax.map(attend, qkv).reshape(-1, D)
    mixed = resid.reshape(-1, D).astype(jnp.float32) + jnp.dot(attended, w_out, preferred_element_type=jnp.float32)
    meansq = lax.optimization_barrier(jnp.mean(mixed * mixed, axis=-1, keepdims=True))
    normed = (mixed * lax.rsqrt(meansq + epsilon) * norm_gain).astype(jnp.bfloat16)
    chosen = expert_ids.reshape(-1, TOPK)
    gate_vals = gate_weights(normed, router_w, chosen)
    point_count = chosen.shape[0]
    blocks = point_count // TOK_DEV
    ranks = slot_ranks(chosen, TOK_DEV, EXPERTS)
    source_block = (jnp.arange(point_count, dtype=jnp.int32) // TOK_DEV)[:, None]
    slot_index = chosen * (blocks * SLOTS) + source_block * SLOTS + ranks
    spread = jnp.broadcast_to(normed[:, None, :], (point_count, TOPK, D)).reshape(-1, D)
    buffers = jnp.zeros((EXPERTS * blocks * SLOTS, D), jnp.bfloat16).at[slot_index.reshape(-1)].set(spread)
    outputs = lax.map(expert_out, (buffers.reshape(EXPERTS, blocks * SLOTS, D), w_gate_up, w_down))
    out_table = outputs.reshape(-1, D)
    expert_sum = lax.optimization_barrier(jnp.sum(gate_vals[:, :, None] * out_table[slot_index], axis=1))
    return (mixed + expert_sum).astype(jnp.bfloat16).reshape(SETS, SET_LEN, D)
```

```python
import math

import jax
import jax.numpy as jnp
from jax import lax
from jax.sharding import PartitionSpec as P

H = 16
HD = 128

epsilon = 1e-05


def gate_table(normed_rows, router_w, chosen):
    logits = jnp.dot(normed_rows, router_w, preferred_element_type=jnp.float32)
    experts = jnp.arange(logits.shape[1], dtype=jnp.int32)
    picked = jnp.any(chosen[:, :, None] == experts[None, None, :], axis=1)
    squashed = jnp.where(picked, jax.nn.sigmoid(logits), 0.0)
    gates = squashed / jnp.sum(squashed, axis=-1, keepdims=True)
    return jnp.where(picked, gates, -1.0)


def on_device(resid, qkv, w_out, norm_gain, router_w, expert_ids, w_gate_up, w_down):
    rows = resid.shape[1]
    width = resid.shape[2]
    seq_size = lax.axis_size("seq")
    exp_size = lax.axis_size("exp")
    set_rows = rows * seq_size
    head_local = H // seq_size
    local_width = head_local * HD
    blocks = seq_size * exp_size
    exp_local = w_gate_up.shape[0]
    experts = router_w.shape[1]
    cap = rows // 8

    packed = qkv.reshape(rows, 3, seq_size, local_width)
    regrouped = lax.all_to_all(packed, "seq", split_axis=2, concat_axis=0, tiled=True)
    q = regrouped[:, 0, 0].reshape(set_rows, head_local, HD)
    k = regrouped[:, 1, 0].reshape(set_rows, head_local, HD)
    v = regrouped[:, 2, 0].reshape(set_rows, head_local, HD)
    scores = jnp.einsum("qhd,khd->hqk", q, k, preferred_element_type=jnp.float32) / math.sqrt(HD)
    probs = jax.nn.softmax(scores, axis=-1).astype(jnp.bfloat16)
    attended = jnp.einsum("hqk,khd->qhd", probs, v, preferred_element_type=jnp.float32)
    attended = attended.astype(jnp.bfloat16).reshape(set_rows, local_width)
    part = jnp.dot(attended, w_out, preferred_element_type=jnp.float32).astype(jnp.bfloat16)
    projected = lax.psum_scatter(part, "seq", scatter_dimension=0, tiled=True)
    mixed = resid[0].astype(jnp.float32) + projected.astype(jnp.float32)
    meansq = jnp.mean(mixed * mixed, axis=-1, keepdims=True)
    normed = (mixed * lax.rsqrt(meansq + epsilon) * norm_gain).astype(jnp.bfloat16)

    chosen = lax.dynamic_slice_in_dim(expert_ids[0], lax.axis_index("seq") * rows, rows, 0)
    gates = gate_table(normed, router_w, chosen)
    high = gates.astype(jnp.bfloat16)
    low = (gates - high.astype(jnp.float32)).astype(jnp.bfloat16)
    sent = jnp.concatenate([normed, high, low], axis=1)
    everyone = lax.all_gather(sent, ("exp", "seq"), axis=0, tiled=True)
    points = everyone[:, :width].reshape(blocks, rows, width)
    first = lax.axis_index("exp") * exp_local
    high = lax.dynamic_slice_in_dim(everyone[:, width : width + experts], first, exp_local, 1)
    low = lax.dynamic_slice_in_dim(everyone[:, width + experts :], first, exp_local, 1)
    gates = (high.astype(jnp.float32) + low.astype(jnp.float32)).reshape(blocks, rows, exp_local)
    named = high.reshape(blocks, rows, exp_local) >= 0
    before = jnp.tril(jnp.ones((rows, rows), jnp.bfloat16), -1)
    ranks = jnp.einsum(
        "rs,bse->ber", before, named.astype(jnp.bfloat16), preferred_element_type=jnp.float32
    ).astype(jnp.int32)
    place = named.transpose(0, 2, 1)[:, :, None, :] & (
        ranks[:, :, None, :] == jnp.arange(cap, dtype=jnp.int32)[None, None, :, None]
    )
    slot_gate = jnp.sum(jnp.where(place, gates.transpose(0, 2, 1)[:, :, None, :], 0.0), axis=-1)
    place = place.astype(jnp.bfloat16).reshape(blocks, exp_local * cap, rows)
    slots = jnp.einsum("bsr,brd->bsd", place, points, preferred_element_type=jnp.float32)
    slots = slots.astype(jnp.bfloat16).reshape(blocks, exp_local, cap, width)
    both = jnp.einsum("bend,edgf->bengf", slots, w_gate_up, preferred_element_type=jnp.float32)
    hidden = (jax.nn.silu(both[:, :, :, 0]) * both[:, :, :, 1]).astype(jnp.bfloat16)
    outs = jnp.einsum("benf,efd->bend", hidden, w_down, preferred_element_type=jnp.float32)
    outs = (outs * slot_gate[..., None]).astype(jnp.bfloat16).reshape(blocks, -1, width)
    sums = jnp.einsum("bsr,bsd->brd", place, outs, preferred_element_type=jnp.float32)
    sums = sums.astype(jnp.bfloat16).reshape(blocks * rows, width)
    expert_sum = lax.psum_scatter(sums, ("exp", "seq"), scatter_dimension=0, tiled=True)
    out = mixed + expert_sum.astype(jnp.float32)
    return out.astype(jnp.bfloat16).reshape(1, rows, width)


def solution(mesh):
    in_specs = (
        P("exp", "seq", None),
        P("exp", "seq", None),
        P("seq", None),
        P(),
        P(),
        P("exp", None, None),
        P("exp", None, None, "seq"),
        P("exp", "seq", None),
    )
    return jax.shard_map(
        on_device,
        mesh=mesh,
        in_specs=in_specs,
        out_specs=P("exp", "seq", None),
        check_vma=False,
    )
```

```python
import functools
import math

import jax
import jax.numpy as jnp
from jax import lax
from jax.experimental import pallas as pl
from jax.experimental.pallas import tpu as pltpu
from jax.sharding import PartitionSpec as P

H = 16
HD = 128

epsilon = 1e-05


def gate_table(normed_rows, router_w, chosen):
    logits = jnp.dot(normed_rows, router_w, preferred_element_type=jnp.float32)
    experts = jnp.arange(logits.shape[1], dtype=jnp.int32)
    picked = jnp.any(chosen[:, :, None] == experts[None, None, :], axis=1)
    squashed = jnp.where(picked, jax.nn.sigmoid(logits), 0.0)
    gates = squashed / jnp.sum(squashed, axis=-1, keepdims=True)
    return jnp.where(picked, gates, -1.0)


MESH = pl.DeviceIdType.MESH


def greet(chips, seq_size):
    exp, seq = lax.axis_index("exp"), lax.axis_index("seq")
    chip, core = exp // 2, exp % 2
    barrier = pltpu.get_barrier_semaphore()
    pl.semaphore_signal(
        barrier, inc=1, device_id={"exp": chip * 2 + 1 - core, "seq": seq}, device_id_type=MESH
    )
    for j in range(1, seq_size):
        pl.semaphore_signal(
            barrier,
            inc=1,
            device_id={"exp": exp, "seq": (seq + j) % seq_size},
            device_id_type=MESH,
        )
    for i in range(1, chips):
        pl.semaphore_signal(
            barrier,
            inc=1,
            device_id={"exp": (chip + i) % chips * 2 + core, "seq": seq},
            device_id_type=MESH,
        )
    pl.semaphore_wait(barrier, seq_size + chips - 1)


def scatter_kernel(
    chips, seq_size, x_ref, out_ref, pair, by_seq, done, by_chip, s0, r0, s1, r1, s2, r2
):
    exp, seq = lax.axis_index("exp"), lax.axis_index("seq")
    chip, core = exp // 2, exp % 2
    rows = out_ref.shape[0]
    step = 16
    parts = rows // step
    greet(chips, seq_size)

    def target(i):
        return (chip + 1 + i) % chips

    def copy(src, dst, send, recv, e, s):
        made = pltpu.make_async_remote_copy(
            src_ref=src,
            dst_ref=dst,
            send_sem=send,
            recv_sem=recv,
            device_id={"exp": e, "seq": s},
            device_id_type=MESH,
        )
        made.start()
        return made

    to_core = [
        copy(
            x_ref.at[target(i) * 2 + 1 - core],
            pair.at[i],
            s0.at[i],
            r0.at[i],
            chip * 2 + 1 - core,
            seq,
        )
        for i in range(chips)
    ]
    to_seq, to_chip = [], []

    def finish(i):
        for c in to_seq[i]:
            c.wait_recv()
        last = i == chips - 1

        @pl.loop(0, parts)
        def _(t):
            at = pl.ds(pl.multiple_of(t * step, step), step)
            total = pair[i, seq, at, :].astype(jnp.float32)
            for j in range(seq_size - 1):
                total += by_seq[j, i, at, :].astype(jnp.float32)
            if last:
                out_ref[at, :] = total
            else:
                done[i, at, :] = total.astype(jnp.bfloat16)

        if not last:
            to_chip.append(
                copy(
                    done.at[i], by_chip.at[i], s2.at[i], r2.at[i], target(i) * 2 + core, seq
                )
            )

    for i in range(chips):
        to_core[i].wait_recv()

        @pl.loop(0, seq_size * parts)
        def _(t):
            p = t // parts
            at = pl.ds(pl.multiple_of(t % parts * step, step), step)
            mine = x_ref[target(i) * 2 + core, p, at, :].astype(jnp.float32)
            pair[i, p, at, :] = (mine + pair[i, p, at, :].astype(jnp.float32)).astype(jnp.bfloat16)

        sends = []
        for j in range(1, seq_size):
            peer = (seq + j) % seq_size
            sends.append(
                copy(
                    pair.at[i, peer],
                    by_seq.at[j - 1, i],
                    s1.at[i, j - 1],
                    r1.at[i, j - 1],
                    exp,
                    peer,
                )
            )
        to_seq.append(sends)
        if i > 0:
            finish(i - 1)
    finish(chips - 1)
    for c in to_chip:
        c.wait_recv()

    @pl.loop(0, parts)
    def _(t):
        at = pl.ds(pl.multiple_of(t * step, step), step)
        total = out_ref[at, :]
        for i in range(chips - 1):
            total += by_chip[i, at, :].astype(jnp.float32)
        out_ref[at, :] = total

    for c in to_core + [c for sends in to_seq for c in sends] + to_chip:
        c.wait_send()


def reduce_blocks(sums, exp_size, seq_size):
    rows, width = sums.shape[2:]
    chips = exp_size // 2
    dma = pltpu.SemaphoreType.DMA
    return pl.pallas_call(
        functools.partial(scatter_kernel, chips, seq_size),
        out_shape=jax.ShapeDtypeStruct((rows, width), jnp.float32),
        in_specs=[pl.BlockSpec(memory_space=pltpu.VMEM)],
        out_specs=pl.BlockSpec(memory_space=pltpu.VMEM),
        scratch_shapes=[
            pltpu.VMEM((chips, seq_size, rows, width), jnp.bfloat16),
            pltpu.VMEM((seq_size - 1, chips, rows, width), jnp.bfloat16),
            pltpu.VMEM((chips - 1, rows, width), jnp.bfloat16),
            pltpu.VMEM((chips - 1, rows, width), jnp.bfloat16),
            dma((chips,)),
            dma((chips,)),
            dma((chips, seq_size - 1)),
            dma((chips, seq_size - 1)),
            dma((chips - 1,)),
            dma((chips - 1,)),
        ],
        compiler_params=pltpu.CompilerParams(
            collective_id=0, has_side_effects=True, vmem_limit_bytes=48 << 20
        ),
    )(sums)


def on_device(resid, qkv, w_out, norm_gain, router_w, expert_ids, w_gate_up, w_down):
    rows = resid.shape[1]
    width = resid.shape[2]
    seq_size = lax.axis_size("seq")
    exp_size = lax.axis_size("exp")
    set_rows = rows * seq_size
    head_local = H // seq_size
    local_width = head_local * HD
    blocks = seq_size * exp_size
    exp_local = w_gate_up.shape[0]
    experts = router_w.shape[1]
    cap = rows // 8

    packed = qkv.reshape(rows, 3, seq_size, local_width)
    regrouped = lax.all_to_all(packed, "seq", split_axis=2, concat_axis=0, tiled=True)
    q = regrouped[:, 0, 0].reshape(set_rows, head_local, HD)
    k = regrouped[:, 1, 0].reshape(set_rows, head_local, HD)
    v = regrouped[:, 2, 0].reshape(set_rows, head_local, HD)
    scores = jnp.einsum("qhd,khd->hqk", q, k, preferred_element_type=jnp.float32) / math.sqrt(HD)
    probs = jax.nn.softmax(scores, axis=-1).astype(jnp.bfloat16)
    attended = jnp.einsum("hqk,khd->qhd", probs, v, preferred_element_type=jnp.float32)
    attended = attended.astype(jnp.bfloat16).reshape(set_rows, local_width)
    part = jnp.dot(attended, w_out, preferred_element_type=jnp.float32).astype(jnp.bfloat16)
    projected = lax.psum_scatter(part, "seq", scatter_dimension=0, tiled=True)
    mixed = resid[0].astype(jnp.float32) + projected.astype(jnp.float32)
    meansq = jnp.mean(mixed * mixed, axis=-1, keepdims=True)
    normed = (mixed * lax.rsqrt(meansq + epsilon) * norm_gain).astype(jnp.bfloat16)

    chosen = lax.dynamic_slice_in_dim(expert_ids[0], lax.axis_index("seq") * rows, rows, 0)
    gates = gate_table(normed, router_w, chosen)
    high = gates.astype(jnp.bfloat16)
    low = (gates - high.astype(jnp.float32)).astype(jnp.bfloat16)
    sent = jnp.concatenate([normed, high, low], axis=1)
    everyone = lax.all_gather(sent, ("exp", "seq"), axis=0, tiled=True)
    points = everyone[:, :width].reshape(blocks, rows, width)
    first = lax.axis_index("exp") * exp_local
    high = lax.dynamic_slice_in_dim(everyone[:, width : width + experts], first, exp_local, 1)
    low = lax.dynamic_slice_in_dim(everyone[:, width + experts :], first, exp_local, 1)
    gates = (high.astype(jnp.float32) + low.astype(jnp.float32)).reshape(blocks, rows, exp_local)
    named = high.reshape(blocks, rows, exp_local) >= 0
    before = jnp.tril(jnp.ones((rows, rows), jnp.bfloat16), -1)
    ranks = jnp.einsum(
        "rs,bse->ber", before, named.astype(jnp.bfloat16), preferred_element_type=jnp.float32
    ).astype(jnp.int32)
    place = named.transpose(0, 2, 1)[:, :, None, :] & (
        ranks[:, :, None, :] == jnp.arange(cap, dtype=jnp.int32)[None, None, :, None]
    )
    slot_gate = jnp.sum(jnp.where(place, gates.transpose(0, 2, 1)[:, :, None, :], 0.0), axis=-1)
    place = place.astype(jnp.bfloat16).reshape(blocks, exp_local * cap, rows)
    slots = jnp.einsum("bsr,brd->bsd", place, points, preferred_element_type=jnp.float32)
    slots = slots.astype(jnp.bfloat16).reshape(blocks, exp_local, cap, width)
    both = jnp.einsum("bend,edgf->bengf", slots, w_gate_up, preferred_element_type=jnp.float32)
    hidden = (jax.nn.silu(both[:, :, :, 0]) * both[:, :, :, 1]).astype(jnp.bfloat16)
    outs = jnp.einsum("benf,efd->bend", hidden, w_down, preferred_element_type=jnp.float32)
    outs = (outs * slot_gate[..., None]).astype(jnp.bfloat16).reshape(blocks, -1, width)
    sums = jnp.einsum("bsr,bsd->brd", place, outs, preferred_element_type=jnp.float32)
    sums = sums.astype(jnp.bfloat16).reshape(blocks * rows, width)
    if exp_size > 8:
        expert_sum = lax.psum_scatter(sums, ("exp", "seq"), scatter_dimension=0, tiled=True)
    else:
        expert_sum = reduce_blocks(
            sums.reshape(exp_size, seq_size, rows, width), exp_size, seq_size
        )
    out = mixed + expert_sum.astype(jnp.float32)
    return out.astype(jnp.bfloat16).reshape(1, rows, width)


def solution(mesh):
    in_specs = (
        P("exp", "seq", None),
        P("exp", "seq", None),
        P("seq", None),
        P(),
        P(),
        P("exp", None, None),
        P("exp", None, None, "seq"),
        P("exp", "seq", None),
    )
    return jax.shard_map(
        on_device,
        mesh=mesh,
        in_specs=in_specs,
        out_specs=P("exp", "seq", None),
        check_vma=False,
    )
```
